32 devices in a mesh: sx: 2 (over y), sy: 4 (over z), af: 4 (over x, core).
Axes of the slice: x: 2, y: 2, z: 4, core: 2. Of those that a mesh axis runs over, the one named last changes fastest.
Arguments:
- sky_maps: float32 [64, 128, 1024], P('sx', 'sy', 'af'), may hold values from -16 to 25
- validity: int32 [64, 128], P('sx', 'sy'), may hold values 0 or 1
- row_taps: float32 [1024, 65], P('af'), may hold values from -0.75 to 0.75
- column_taps: float32 [1024, 65], P('af'), may hold values from -0.75 to 0.75
- init_loadings: float32 [1024, 32], P('af'), may hold values from -0.1875 to 0.1875
Outputs:
- cleaned_maps: float32 [64, 128, 1024], P('sx', 'sy', 'af')
- loadings: float32 [1024, 32], P('af')
- noise_var: float32 [], replicated
The draws below stay inside these ranges and needn't reach their ends.
All inputs are finite; a program needn't handle non-finite values. No bound on the sum of `validity` on one device may be relied on, other than what follows from the above.
Results may differ from the reference program's by a relative error of at most 0.0003.
Values sent between devices are 32-bit elements; how exact they have to be, the bound alone decides.
A program may use at most 128 MiB of HBM per device.

```python
import math
import jax
import jax.numpy as jnp
from jax import lax

FREQS = 1024
COMPONENTS = 32
TAPS = 65
ITERS = 4
HALO = 32
NR = 64
NC = 128
NPIX = 8192


def draw_sky_maps(key, part):
    subkeys = jax.random.split(key, 5)
    pixel_shape = (NR, NC, 1)
    row_place = jnp.arange(NR, dtype=jnp.float32)[:, None, None]
    frequency = jnp.arange(FREQS, dtype=jnp.float32)[None, None, :]
    log_ratio = jnp.log(1.0 + frequency / FREQS)
    spread = 0.7
    noise_part = jnp.clip(jax.random.normal(subkeys[0], (NR, NC, FREQS), jnp.float32), -5.0, 5.0)
    gradient = jnp.exp(jnp.log(3.0) * row_place / NR)
    first_amp = jnp.exp(jax.random.uniform(subkeys[1], pixel_shape, jnp.float32, -spread, spread))
    first_index = jax.random.uniform(subkeys[2], pixel_shape, jnp.float32, 2.4, 3.0)
    second_amp = jnp.exp(jax.random.uniform(subkeys[3], pixel_shape, jnp.float32, -spread, spread))
    second_index = jax.random.uniform(subkeys[4], pixel_shape, jnp.float32, 1.9, 2.2)
    foreground = first_amp * jnp.exp(-first_index * log_ratio) + 0.6 * second_amp * jnp.exp(-second_index * log_ratio)
    return (gradient * (foreground + noise_part)).astype(jnp.float32)


def touch_ends(entries, rng, low, top_value):
    longest = entries.shape.index(max(entries.shape))
    spots = []
    for shift in (0, 1):
        where = [jax.random.randint(jax.random.fold_in(rng, axis), (), 0, length) for axis, length in enumerate(entries.shape)]
        where[longest] = (where[longest] + shift) % entries.shape[longest]
        spots.append(tuple(where))
    return entries.at[spots[0]].set(low).at[spots[1]].set(top_value)


def shard_levels(rng, shape, cuts, least, top_value):
    gain, own = 1.0, jax.random.fold_in(rng, 6)
    for dim, blocks in cuts:
        steps = jnp.exp(jax.random.uniform(jax.random.fold_in(own, dim), (blocks,), jnp.float32, least / len(cuts), top_value / len(cuts)))
        gain = gain * jnp.repeat(steps, shape[dim] // blocks).reshape([-1 if axis == dim else 1 for axis in range(len(shape))])
    return gain


def gaussian(own_key, shape, deviation, reach, cuts=(), kind=jnp.bfloat16):
    values = jax.random.normal(own_key, shape, jnp.float32) * deviation
    if len(cuts) > 0:
        values = shard_levels(own_key, shape, cuts, -0.22, 0.18) * values
    return jnp.clip(values, min=-reach, max=reach).astype(kind)


def setup_inputs(seed: int = 0) -> dict:
    key_list = jax.random.split(jax.random.key(seed), 6)
    return {
        "sky_maps": draw_sky_maps(jax.random.fold_in(key_list[5], 71), 0),
        "validity": touch_ends((jax.random.randint(key_list[1], (NR, NC), 0, 8) < 7).astype(jnp.int32), jax.random.fold_in(key_list[1], 1), 0, 1),
        "row_taps": gaussian(key_list[2], (FREQS, TAPS), TAPS ** -0.5, 0.75, ((0, 4),), jnp.float32),
        "column_taps": gaussian(key_list[3], (FREQS, TAPS), TAPS ** -0.5, 0.75, ((0, 4),), jnp.float32),
        "init_loadings": gaussian(key_list[4], (FREQS, COMPONENTS), FREQS ** -0.5, 0.1875, ((0, 4),), jnp.float32),
    }


HIGHEST_PRECISION = lax.Precision.HIGHEST

def inverse_spd(matrix):
    identity = jnp.eye(matrix.shape[0], dtype=matrix.dtype)
    factor = jnp.linalg.cholesky(matrix)
    lower_inverse = lax.linalg.triangular_solve(factor, identity, left_side=True, lower=True)
    return jnp.dot(lower_inverse.T, lower_inverse, precision=HIGHEST_PRECISION)

def reference(sky_maps, validity, row_taps, column_taps, init_loadings):
    masked = sky_maps * validity.astype(jnp.float32)[:, :, None]
    block_size = math.gcd(FREQS, 16)

    def beam_block(first_freq):
        slab_part = lax.dynamic_slice_in_dim(masked, first_freq, block_size, 2)
        row_block = lax.dynamic_slice_in_dim(row_taps, first_freq, block_size, 0)
        column_block = lax.dynamic_slice_in_dim(column_taps, first_freq, block_size, 0)
        padded = jnp.pad(slab_part, ((HALO, HALO), (0, 0), (0, 0)))
        smoothed = jnp.zeros_like(slab_part)
        for tap_place in range(TAPS):
            smoothed = smoothed + row_block[:, tap_place] * padded[tap_place:tap_place + NR]
        padded = jnp.pad(smoothed, ((0, 0), (HALO, HALO), (0, 0)))
        beamed = jnp.zeros_like(slab_part)
        for tap_place in range(TAPS):
            beamed = beamed + column_block[:, tap_place] * padded[:, tap_place:tap_place + NC]
        return beamed
    starts = jnp.arange(FREQS // block_size, dtype=jnp.int32) * block_size
    stacked = lax.map(beam_block, starts)
    spectra = jnp.moveaxis(stacked, 0, 2).reshape(NPIX, FREQS)
    total_power = jnp.sum(spectra * spectra)
    identity = jnp.eye(COMPONENTS, dtype=jnp.float32)
    loadings = init_loadings
    noise_var = jnp.float32(1.0)
    for iteration in range(ITERS):
        gram_matrix = jnp.dot(loadings.T, loadings, precision=HIGHEST_PRECISION)
        inverse = inverse_spd(gram_matrix + noise_var * identity)
        latent = jnp.dot(spectra, jnp.dot(loadings, inverse, precision=HIGHEST_PRECISION), precision=HIGHEST_PRECISION)
        cross_moment = jnp.dot(spectra.T, latent, precision=HIGHEST_PRECISION)
        second = jnp.dot(latent.T, latent, precision=HIGHEST_PRECISION)
        scaled = NPIX * noise_var * inverse + second
        updated = jnp.dot(cross_moment, inverse_spd(scaled), precision=HIGHEST_PRECISION)
        new_gram = jnp.dot(updated.T, updated, precision=HIGHEST_PRECISION)
        noise_var = (total_power - 2.0 * jnp.sum(updated * cross_moment) + jnp.sum(scaled * new_gram)) / (NPIX * FREQS)
        loadings = updated
    gram_matrix = jnp.dot(loadings.T, loadings, precision=HIGHEST_PRECISION)
    inverse = inverse_spd(gram_matrix + noise_var * identity)
    latent = jnp.dot(spectra, jnp.dot(loadings, inverse, precision=HIGHEST_PRECISION), precision=HIGHEST_PRECISION)
    cleaned = spectra - jnp.dot(latent, loadings.T, precision=HIGHEST_PRECISION)
    return (cleaned.reshape(NR, NC, FREQS), loadings, noise_var)
```

```python
import functools

import jax
import jax.numpy as jnp
from jax import lax
from jax.experimental import pallas as pl
from jax.experimental.pallas import tpu as pltpu
from jax.sharding import PartitionSpec as P

ITERS = 4
EXACT = lax.Precision.HIGHEST
MESH = pl.DeviceIdType.MESH
F32 = jnp.float32


def dot_nn(left, right):
    return lax.dot_general(
        left, right, (((1,), (0,)), ((), ())), precision=EXACT, preferred_element_type=F32
    )


def dot_nt(left, right):
    return lax.dot_general(
        left, right, (((1,), (1,)), ((), ())), precision=EXACT, preferred_element_type=F32
    )


def inverse_spd(matrix):
    size = matrix.shape[0]
    sub = lax.broadcasted_iota(jnp.int32, (size, size), 0)
    lane = lax.broadcasted_iota(jnp.int32, (size, size), 1)
    for k in range(size):
        pivot = 1.0 / matrix[k : k + 1, k : k + 1]
        row = jnp.where(lane[:1] == k, pivot, matrix[k : k + 1, :] * pivot)
        col = matrix[:, k : k + 1]
        matrix = jnp.where(sub == k, row, jnp.where(lane == k, 0.0, matrix) - col * row)
    return matrix


def kernel(
    sizes, x_ref, rt_ref, ct_ref, l0_ref,
    out_ref, lout_ref, nv_ref,
    ext, cext, wr, wc, beamed, sp, lt, part, rsbuf, agbuf, mine, tpown, tpbuf, latg,
    y_send, y_recv, z_send, z_recv, l_send, l_recv, a_send, a_recv,
    tp_send, tp_recv, rs_send, rs_recv, ag_send, ag_recv, lat_send, lat_recv,
):
    nsx, nsy, naf = sizes
    ndev = nsx * nsy * naf
    rows, cols, freqs = x_ref.shape
    taps = rt_ref.shape[0]
    comps = l0_ref.shape[0]
    halo = (taps - 1) // 2
    fblocks = freqs // 128
    cgroups = cols // 8
    grows = rows // naf
    gpix = grows * cols
    pixels = rows * cols * nsx * nsy
    ftotal = freqs * naf
    tile_rows, tile_cols = comps // 8, ftotal // 128
    tiles = tile_rows * tile_cols

    sx, sy, af = lax.axis_index("sx"), lax.axis_index("sy"), lax.axis_index("af")
    me = (sx * nsy + sy) * naf + af

    def coords(flat):
        return (
            lax.div(flat, nsy * naf), lax.rem(lax.div(flat, naf), nsy), lax.rem(flat, naf)
        )

    barrier = pltpu.get_barrier_semaphore()

    def greet(k, carry):
        pl.semaphore_signal(
            barrier, inc=1, device_id=coords(lax.rem(me + k, ndev)), device_id_type=MESH
        )
        return carry

    lax.fori_loop(1, ndev, greet, 0)
    pl.semaphore_wait(barrier, ndev - 1)

    chunks = [(fb, cg) for fb in range(fblocks) for cg in range(cgroups)]

    def remote(src, dst, send, recv, target):
        return pltpu.make_async_remote_copy(
            src_ref=src, dst_ref=dst, send_sem=send, recv_sem=recv,
            device_id=target, device_id_type=MESH,
        )

    def y_copy(way, fb, cg):
        n = fb * cgroups + cg
        low = 0 if way == 0 else rows + halo
        return remote(
            x_ref.at[:, pl.ds(8 * cg, 8), pl.ds(128 * fb, 128)],
            ext.at[pl.ds(low, rows), pl.ds(8 * cg, 8), pl.ds(128 * fb, 128)],
            y_send.at[way, n], y_recv.at[way, n],
            (sx + 1 if way == 0 else sx - 1, sy, af),
        )

    def z_copy(way, fb, cg):
        n = fb * cgroups + cg
        low = 0 if way == 0 else cols + halo
        return remote(
            cext.at[:, pl.ds(halo + 8 * cg, 8), pl.ds(128 * fb, 128)],
            cext.at[:, pl.ds(low + 8 * cg, 8), pl.ds(128 * fb, 128)],
            z_send.at[way, n], z_recv.at[way, n],
            (sx, sy + 1 if way == 0 else sy - 1, af),
        )

    y_out = (sx < nsx - 1, sx > 0)
    y_in = (sx > 0, sx < nsx - 1)
    z_out = (sy < nsy - 1, sy > 0)
    z_in = (sy > 0, sy < nsy - 1)

    for way in range(2):
        @pl.when(y_out[way])
        def _():
            for fb, cg in chunks:
                y_copy(way, fb, cg).start()

    def l_copy(k):
        return remote(
            l0_ref, lt.at[af], l_send.at[k - 1], l_recv.at[k - 1],
            (sx, sy, lax.rem(af + k, naf)),
        )

    for k in range(1, naf):
        l_copy(k).start()
    lt[af] = l0_ref[...]

    for way in range(2):
        low = 0 if way == 0 else rows + halo

        @pl.when(jnp.logical_not(y_in[way]))
        def _():
            ext[pl.ds(low, halo)] = jnp.zeros((halo, cols, freqs), F32)

        @pl.when(jnp.logical_not(z_in[way]))
        def _():
            clow = 0 if way == 0 else cols + halo
            for r in range(rows):
                cext[r, pl.ds(clow, halo), :] = jnp.zeros((halo, freqs), F32)

    ext[pl.ds(halo, rows)] = x_ref[...]
    for t in range(taps):
        wr[t] = jnp.broadcast_to(rt_ref[pl.ds(t, 1), :], (8, freqs))
        wc[t] = jnp.broadcast_to(ct_ref[pl.ds(t, 1), :], (8, freqs))

    for fb, cg in chunks:
        n = fb * cgroups + cg
        for way in range(2):
            @pl.when(y_in[way])
            def _():
                y_copy(way, fb, cg).wait_recv()
        cs, fs = pl.ds(8 * cg, 8), pl.ds(128 * fb, 128)

        def add_tap(t, acc):
            return acc + wr[t, :, fs][None] * ext[pl.ds(t, rows), cs, fs]

        acc = lax.fori_loop(0, taps, add_tap, jnp.zeros((rows, 8, 128), F32))
        cext[:, pl.ds(halo + 8 * cg, 8), fs] = acc
        for way in range(2):
            @pl.when(z_out[way])
            def _():
                z_copy(way, fb, cg).start()

    def a_copy(k, fb):
        g = lax.rem(af + k, naf)
        return remote(
            beamed.at[pl.ds(g * gpix, gpix), pl.ds(128 * fb, 128)],
            sp.at[af, :, pl.ds(128 * fb, 128)],
            a_send.at[k - 1, fb], a_recv.at[k - 1, fb], (sx, sy, g),
        )

    power = jnp.zeros((8, 128), F32)
    for fb in range(fblocks):
        fs = pl.ds(128 * fb, 128)
        for way in range(2):
            @pl.when(z_in[way])
            def _():
                for cg in range(cgroups):
                    z_copy(way, fb, cg).wait_recv()
        for k in range(1, naf + 1):
            g = lax.rem(af + k, naf)

            def one_row(i, power):
                r = g * grows + i
                wide = cols // 8 + 1
                strip = cext[r, :, fs].reshape((cols + 2 * halo) // 8, 8, 128)
                total = jnp.zeros((cols, 128), F32)
                for s in range(8):
                    y = None
                    for t in range(s, taps, 8):
                        q = t // 8
                        if q + wide > strip.shape[0]:
                            last = strip[q : q + wide - 1] * wc[t, :, fs][None]
                            total = total + last.reshape(cols, 128)
                            continue
                        term = strip[q : q + wide] * wc[t, :, fs][None]
                        y = term if y is None else y + term
                    total = total + y.reshape(8 * wide, 128)[s : s + cols]
                beamed[pl.ds(pl.multiple_of(r * cols, 8), cols), fs] = total
                return power + jnp.sum((total * total).reshape(cols // 8, 8, 128), axis=0)

            power = lax.fori_loop(0, grows, one_row, power)
            if k < naf:
                a_copy(k, fb).start()
            else:
                sp[af, :, fs] = beamed[pl.ds(pl.multiple_of(af * gpix, 8), gpix), fs]

    def all_pairs(make):
        def step(k, carry):
            make(k).start()
            return carry
        lax.fori_loop(1, ndev, step, 0)

    tpown[...] = power
    tpbuf[me] = power
    all_pairs(lambda k: remote(
        tpown, tpbuf.at[me], tp_send, tp_recv, coords(lax.rem(me + k, ndev))
    ))
    for k in range(1, naf):
        l_copy(k).wait_recv()
        for fb in range(fblocks):
            a_copy(k, fb).wait_recv()

    def wide_of(ref):
        return jnp.concatenate([ref[a] for a in range(naf)], axis=1)

    eye = (
        lax.broadcasted_iota(jnp.int32, (comps, comps), 0)
        == lax.broadcasted_iota(jnp.int32, (comps, comps), 1)
    ).astype(F32)

    def latent_of(at):
        total = None
        for a in range(naf):
            term = dot_nt(at[:, freqs * a : freqs * (a + 1)], sp[a])
            total = term if total is None else total + term
        return total

    def pieces(ref, count):
        return ref.at[pl.ds(0, count)]

    def wait_all(ref, count, send, recv):
        return remote(pieces(ref, count), pieces(ref, count), send, recv, (sx, sy, af))

    wait_all(tpbuf, ndev - 1, tp_send, tp_recv).wait_recv()
    power = lax.fori_loop(1, ndev, lambda k, acc: acc + tpbuf[k], tpbuf[0])
    total_power = jnp.sum(jnp.sum(power, axis=1, keepdims=True), axis=0, keepdims=True)
    wait_all(tpbuf, ndev - 1, tp_send, tp_recv).wait_send()

    def total_of(value):
        return jnp.sum(jnp.sum(value, axis=1, keepdims=True), axis=0, keepdims=True)

    def em_step(iteration, carry):
        gram, noise = carry
        loadings = wide_of(lt)
        inverse = inverse_spd(gram + noise * eye)
        at = dot_nn(inverse, loadings)
        latent = latent_of(at)
        for a in range(naf):
            cross = dot_nn(latent, sp[a])
            for i in range(tile_rows):
                for j in range(freqs // 128):
                    part[i * tile_cols + a * (freqs // 128) + j] = cross[
                        8 * i : 8 * i + 8, 128 * j : 128 * j + 128
                    ]

        def scatter(k, carry):
            owner = lax.rem(me + k, ndev)

            @pl.when(owner < tiles)
            def _():
                remote(
                    part.at[owner], rsbuf.at[k - 1], rs_send, rs_recv, coords(owner)
                ).start()

            return carry

        lax.fori_loop(1, ndev, scatter, 0)

        @pl.when(me < tiles)
        def _():
            wait_all(rsbuf, ndev - 1, rs_send, rs_recv).wait_recv()
            full = lax.fori_loop(
                0, ndev - 1, lambda k, acc: acc + rsbuf[k], part[me], unroll=False
            )
            mine[...] = full
            agbuf[me] = full
            all_pairs(lambda k: remote(
                mine, agbuf.at[me], ag_send, ag_recv, coords(lax.rem(me + k, ndev))
            ))
            wait_all(agbuf, tiles - 1, ag_send, ag_recv).wait_recv()
            wait_all(part, tiles - 1, rs_send, rs_recv).wait_send()
            wait_all(rsbuf, ndev - 1, ag_send, ag_recv).wait_send()

        if ndev > tiles:
            @pl.when(me >= tiles)
            def _():
                wait_all(agbuf, tiles, ag_send, ag_recv).wait_recv()
                wait_all(part, tiles, rs_send, rs_recv).wait_send()

        cross = jnp.concatenate(
            [
                jnp.concatenate([agbuf[i * tile_cols + j] for j in range(tile_cols)], axis=1)
                for i in range(tile_rows)
            ],
            axis=0,
        )
        second = dot_nt(cross, at)
        scaled = (pixels * noise) * inverse + second
        updated = dot_nn(inverse_spd(scaled), cross)
        gram = dot_nt(updated, updated)
        trace = total_of(updated * cross)
        noise = (total_power - 2.0 * trace + total_of(scaled * gram)) / (pixels * ftotal)
        for a in range(naf):
            lt[a] = updated[:, freqs * a : freqs * (a + 1)]
        return gram, noise

    start = wide_of(lt)
    gram, noise = lax.fori_loop(
        0, ITERS, em_step, (dot_nt(start, start), jnp.ones((1, 1), F32))
    )
    nv_ref[...] = noise
    lout_ref[...] = lt[af]
    latent = latent_of(dot_nn(inverse_spd(gram + noise * eye), wide_of(lt)))
    latg[af] = latent

    def lat_copy(k):
        return remote(
            latg.at[af], latg.at[af], lat_send.at[k - 1], lat_recv.at[k - 1],
            (sx, sy, lax.rem(af + k, naf)),
        )

    for k in range(1, naf):
        lat_copy(k).start()
    for k in range(naf):
        if k > 0:
            lat_copy(k).wait_recv()
        g = lax.rem(af - k + naf, naf)
        span = pl.ds(pl.multiple_of(g * gpix, 8), gpix)
        out_ref[span, :] = beamed[span, :] - dot_nn(latg[g].T, lt[af])

    for way in range(2):
        @pl.when(y_out[way])
        def _():
            for fb, cg in chunks:
                y_copy(way, fb, cg).wait_send()

        @pl.when(z_out[way])
        def _():
            for fb, cg in chunks:
                z_copy(way, fb, cg).wait_send()
    for k in range(1, naf):
        l_copy(k).wait_send()
        lat_copy(k).wait_send()
        for fb in range(fblocks):
            a_copy(k, fb).wait_send()


def body(sizes, sky_maps, validity, row_taps, column_taps, init_loadings):
    rows, cols, freqs = sky_maps.shape
    comps = init_loadings.shape[1]
    taps = row_taps.shape[1]
    halo = (taps - 1) // 2
    nsx, nsy, naf = sizes
    ndev = nsx * nsy * naf
    tiles = (comps // 8) * (freqs * naf // 128)
    masked = sky_maps * validity.astype(F32)[:, :, None]
    vmem = pl.BlockSpec(memory_space=pltpu.VMEM)
    dma = pltpu.SemaphoreType.DMA
    count = (freqs // 128) * (cols // 8)
    cleaned, loadings, noise = pl.pallas_call(
        functools.partial(kernel, sizes),
        out_shape=(
            jax.ShapeDtypeStruct((rows * cols, freqs), F32),
            jax.ShapeDtypeStruct((comps, freqs), F32),
            jax.ShapeDtypeStruct((1, 1), F32),
        ),
        in_specs=[vmem] * 4,
        out_specs=(vmem, vmem, vmem),
        scratch_shapes=[
            pltpu.VMEM((rows + 2 * halo, cols, freqs), F32),
            pltpu.VMEM((rows, cols + 2 * halo, freqs), F32),
            pltpu.VMEM((taps, 8, freqs), F32),
            pltpu.VMEM((taps, 8, freqs), F32),
            pltpu.VMEM((rows * cols, freqs), F32),
            pltpu.VMEM((naf, rows * cols // naf, freqs), F32),
            pltpu.VMEM((naf, comps, freqs), F32),
            pltpu.VMEM((tiles, 8, 128), F32),
            pltpu.VMEM((ndev, 8, 128), F32),
            pltpu.VMEM((tiles, 8, 128), F32),
            pltpu.VMEM((8, 128), F32),
            pltpu.VMEM((8, 128), F32),
            pltpu.VMEM((ndev, 8, 128), F32),
            pltpu.VMEM((naf, comps, rows * cols // naf), F32),
            dma((2, count)), dma((2, count)), dma((2, count)), dma((2, count)),
            dma((naf - 1,)), dma((naf - 1,)),
            dma((naf - 1, freqs // 128)), dma((naf - 1, freqs // 128)),
            dma, dma, dma, dma, dma, dma,
            dma((naf - 1,)), dma((naf - 1,)),
        ],
        compiler_params=pltpu.CompilerParams(
            collective_id=0, has_side_effects=True, vmem_limit_bytes=48 * 1024 * 1024
        ),
        name="beam_pca",
    )(masked, row_taps.T, column_taps.T, init_loadings.T)
    return cleaned.reshape(rows, cols, freqs), loadings.T, noise[0, 0]


def solution(mesh):
    sizes = tuple(mesh.shape[axis] for axis in ("sx", "sy", "af"))
    placed = (P("sx", "sy", "af"), P("sx", "sy"), P("af", None), P("af", None), P("af", None))
    return jax.shard_map(
        functools.partial(body, sizes),
        mesh=mesh,
        in_specs=placed,
        out_specs=(P("sx", "sy", "af"), P("af", None), P()),
        check_vma=False,
    )
```

```python
import functools

import jax
import jax.numpy as jnp
from jax import lax
from jax.experimental import pallas as pl
from jax.experimental.pallas import tpu as pltpu
from jax.sharding import PartitionSpec as P

ITERS = 4
EXACT = lax.Precision.HIGHEST
MESH = pl.DeviceIdType.MESH
F32 = jnp.float32


def dot_nn(left, right):
    return lax.dot_general(
        left, right, (((1,), (0,)), ((), ())), precision=EXACT, preferred_element_type=F32
    )


def dot_nt(left, right):
    return lax.dot_general(
        left, right, (((1,), (1,)), ((), ())), precision=EXACT, preferred_element_type=F32
    )


def inverse_spd(matrix):
    size, step = matrix.shape[0], 4
    sub = lax.broadcasted_iota(jnp.int32, (size, size), 0)
    lane = lax.broadcasted_iota(jnp.int32, (size, size), 1)
    lane8 = lane[:8]
    for k in range(0, size, step):
        span = range(step)
        rows = [jnp.broadcast_to(matrix[k + i : k + i + 1, :], (8, size)) for i in span]
        cols = [jnp.broadcast_to(matrix[:, k + j : k + j + 1], (size, size)) for j in span]
        small = [
            [jnp.broadcast_to(cols[j][k + i : k + i + 1, :], (8, size)) for j in span]
            for i in span
        ]
        for m in span:
            pivot = 1.0 / small[m][m]
            line = [pivot if j == m else small[m][j] * pivot for j in span]
            small = [
                line if i == m else [
                    (0.0 if j == m else small[i][j]) - small[i][m] * line[j] for j in span
                ]
                for i in span
            ]
        inside = jnp.logical_and(lane >= k, lane < k + step)
        fresh = jnp.where(inside, 0.0, matrix)
        lines = []
        for i in span:
            line = sum(small[i][j] * rows[j] for j in span)
            for j in span:
                line = jnp.where(lane8 == k + j, small[i][j], line)
            line = jnp.concatenate([line] * (size // 8), axis=0)
            fresh = fresh - cols[i] * line
            lines.append(line)
        for i in span:
            fresh = jnp.where(sub == k + i, lines[i], fresh)
        matrix = fresh
    return matrix


def kernel(
    sizes, x_ref, rt_ref, ct_ref, l0_ref,
    out_ref, lout_ref, nv_ref,
    ext, cext, wr, wc, beamed, sp, lt, part, rsbuf, agbuf, mine, tpown, tpbuf, latg, crossbuf,
    y_send, y_recv, z_send, z_recv, l_send, l_recv, a_send, a_recv,
    tp_send, tp_recv, rs_send, rs_recv, ag_send, ag_recv, lat_send, lat_recv,
):
    nsx, nsy, naf = sizes
    ndev = nsx * nsy * naf
    rows, cols, freqs = x_ref.shape
    taps = rt_ref.shape[0]
    comps = l0_ref.shape[0]
    halo = (taps - 1) // 2
    fblocks = freqs // 128
    cgroups = cols // 8
    grows = rows // naf
    gpix = grows * cols
    pixels = rows * cols * nsx * nsy
    ftotal = freqs * naf
    tile_rows, tile_cols = comps // 8, ftotal // 128
    tiles = tile_rows * tile_cols

    sx, sy, af = lax.axis_index("sx"), lax.axis_index("sy"), lax.axis_index("af")
    me = (sx * nsy + sy) * naf + af

    sx_at = [lax.rem(sx + i, nsx) for i in range(nsx)]
    sy_at = [lax.rem(sy + i, nsy) for i in range(nsy)]
    af_at = [lax.rem(af + i, naf) for i in range(naf)]
    peers = [
        (x, y, z) for x in sx_at for y in sy_at for z in af_at
    ][1:]

    barrier = pltpu.get_barrier_semaphore()

    for peer in peers:
        pl.semaphore_signal(barrier, inc=1, device_id=peer, device_id_type=MESH)
    pl.semaphore_wait(barrier, ndev - 1)

    chunks = [(fb, cg) for fb in range(fblocks) for cg in range(cgroups)]

    def remote(src, dst, send, recv, target):
        return pltpu.make_async_remote_copy(
            src_ref=src, dst_ref=dst, send_sem=send, recv_sem=recv,
            device_id=target, device_id_type=MESH,
        )

    def y_copy(way, fb, cg):
        n = fb * cgroups + cg
        low = 0 if way == 0 else rows + halo
        return remote(
            x_ref.at[:, pl.ds(8 * cg, 8), pl.ds(128 * fb, 128)],
            ext.at[pl.ds(low, rows), pl.ds(8 * cg, 8), pl.ds(128 * fb, 128)],
            y_send.at[way, n], y_recv.at[way, n],
            (sx + 1 if way == 0 else sx - 1, sy, af),
        )

    def z_copy(way, fb, cg):
        n = fb * cgroups + cg
        low = 0 if way == 0 else cols + halo
        return remote(
            cext.at[:, pl.ds(halo + 8 * cg, 8), pl.ds(128 * fb, 128)],
            cext.at[:, pl.ds(low + 8 * cg, 8), pl.ds(128 * fb, 128)],
            z_send.at[way, n], z_recv.at[way, n],
            (sx, sy + 1 if way == 0 else sy - 1, af),
        )

    y_out = (sx < nsx - 1, sx > 0)
    y_in = (sx > 0, sx < nsx - 1)
    z_out = (sy < nsy - 1, sy > 0)
    z_in = (sy > 0, sy < nsy - 1)

    for way in range(2):
        @pl.when(y_out[way])
        def _():
            for fb, cg in chunks:
                y_copy(way, fb, cg).start()

    def l_copy(k):
        return remote(
            l0_ref, lt.at[af], l_send.at[k - 1], l_recv.at[k - 1],
            (sx, sy, lax.rem(af + k, naf)),
        )

    for k in range(1, naf):
        l_copy(k).start()
    lt[af] = l0_ref[...]

    for way in range(2):
        low = 0 if way == 0 else rows + halo

        @pl.when(jnp.logical_not(y_in[way]))
        def _():
            ext[pl.ds(low, halo)] = jnp.zeros((halo, cols, freqs), F32)

        @pl.when(jnp.logical_not(z_in[way]))
        def _():
            clow = 0 if way == 0 else cols + halo
            for r in range(rows):
                cext[r, pl.ds(clow, halo), :] = jnp.zeros((halo, freqs), F32)

    ext[pl.ds(halo, rows)] = x_ref[...]
    for t in range(taps):
        wr[t] = jnp.broadcast_to(rt_ref[pl.ds(t, 1), :], (8, freqs))
        wc[t] = jnp.broadcast_to(ct_ref[pl.ds(t, 1), :], (8, freqs))

    for fb, cg in chunks:
        n = fb * cgroups + cg
        for way in range(2):
            @pl.when(y_in[way])
            def _():
                y_copy(way, fb, cg).wait_recv()
        cs, fs = pl.ds(8 * cg, 8), pl.ds(128 * fb, 128)

        def add_tap(t, acc):
            return acc + wr[t, :, fs][None] * ext[pl.ds(t, rows), cs, fs]

        acc = lax.fori_loop(0, taps, add_tap, jnp.zeros((rows, 8, 128), F32))
        cext[:, pl.ds(halo + 8 * cg, 8), fs] = acc
        for way in range(2):
            @pl.when(z_out[way])
            def _():
                z_copy(way, fb, cg).start()

    def a_copy(k, fb):
        g = lax.rem(af + k, naf)
        return remote(
            beamed.at[pl.ds(g * gpix, gpix), pl.ds(128 * fb, 128)],
            sp.at[af, :, pl.ds(128 * fb, 128)],
            a_send.at[k - 1, fb], a_recv.at[k - 1, fb], (sx, sy, g),
        )

    power = jnp.zeros((8, 128), F32)
    for fb in range(fblocks):
        fs = pl.ds(128 * fb, 128)
        for way in range(2):
            @pl.when(z_in[way])
            def _():
                for cg in range(cgroups):
                    z_copy(way, fb, cg).wait_recv()
        for k in range(1, naf + 1):
            g = lax.rem(af + k, naf)

            def one_row(i, power):
                r = g * grows + i
                wide = cols // 8 + 1
                strip = cext[r, :, fs].reshape((cols + 2 * halo) // 8, 8, 128)
                total = jnp.zeros((cols, 128), F32)
                for s in range(8):
                    y = None
                    for t in range(s, taps, 8):
                        q = t // 8
                        if q + wide > strip.shape[0]:
                            last = strip[q : q + wide - 1] * wc[t, :, fs][None]
                            total = total + last.reshape(cols, 128)
                            continue
                        term = strip[q : q + wide] * wc[t, :, fs][None]
                        y = term if y is None else y + term
                    total = total + y.reshape(8 * wide, 128)[s : s + cols]
                beamed[pl.ds(pl.multiple_of(r * cols, 8), cols), fs] = total
                return power + jnp.sum((total * total).reshape(cols // 8, 8, 128), axis=0)

            power = lax.fori_loop(0, grows, one_row, power)
            if k < naf:
                a_copy(k, fb).start()
            else:
                sp[af, :, fs] = beamed[pl.ds(pl.multiple_of(af * gpix, 8), gpix), fs]

    def all_pairs(src, dst, send, recv):
        for peer in peers:
            remote(src, dst, send, recv, peer).start()

    tpown[...] = power
    tpbuf[me] = power
    all_pairs(tpown, tpbuf.at[me], tp_send, tp_recv)
    crossbuf[...] = jnp.zeros((comps, ftotal), F32)
    for k in range(1, naf):
        l_copy(k).wait_recv()
        for fb in range(fblocks):
            a_copy(k, fb).wait_recv()

    def wide_of(ref):
        return jnp.concatenate([ref[a] for a in range(naf)], axis=1)

    eye = (
        lax.broadcasted_iota(jnp.int32, (comps, comps), 0)
        == lax.broadcasted_iota(jnp.int32, (comps, comps), 1)
    ).astype(F32)

    def latent_of(at):
        total = None
        for a in range(naf):
            term = dot_nt(at[:, freqs * a : freqs * (a + 1)], sp[a])
            total = term if total is None else total + term
        return total

    def pieces(ref, count):
        return ref.at[pl.ds(0, count)]

    def wait_all(ref, count, send, recv):
        return remote(pieces(ref, count), pieces(ref, count), send, recv, (sx, sy, af))

    wait_all(tpbuf, ndev - 1, tp_send, tp_recv).wait_recv()
    power = lax.fori_loop(1, ndev, lambda k, acc: acc + tpbuf[k], tpbuf[0])
    total_power = jnp.sum(jnp.sum(power, axis=1, keepdims=True), axis=0, keepdims=True)
    wait_all(tpbuf, ndev - 1, tp_send, tp_recv).wait_send()

    def total_of(value):
        return jnp.sum(jnp.sum(value, axis=1, keepdims=True), axis=0, keepdims=True)

    def noise_of():
        fitted = total_of(wide_of(lt) * crossbuf[...])
        return (total_power - fitted) / (pixels * ftotal)

    def gather():
        wait_all(rsbuf, ndev - 1, rs_send, rs_recv).wait_recv()
        full = part[me]
        for k in range(min(ndev, 32) - 1):
            full = full + rsbuf[k]
        if ndev > 32:
            full = lax.fori_loop(31, ndev - 1, lambda k, acc: acc + rsbuf[k], full)
        mine[...] = full
        agbuf[me] = full
        all_pairs(mine, agbuf.at[me], ag_send, ag_recv)
        wait_all(agbuf, tiles - 1, ag_send, ag_recv).wait_recv()
        wait_all(part, tiles - 1, rs_send, rs_recv).wait_send()
        wait_all(rsbuf, ndev - 1, ag_send, ag_recv).wait_send()

    def em_step(iteration, carry):
        latent = latent_of(wide_of(lt))
        for a in range(naf):
            cross = dot_nn(latent, sp[a])
            for i in range(tile_rows):
                for j in range(freqs // 128):
                    part[i * tile_cols + a * (freqs // 128) + j] = cross[
                        8 * i : 8 * i + 8, 128 * j : 128 * j + 128
                    ]
        for k, peer in enumerate(peers):
            owner = (peer[0] * nsy + peer[1]) * naf + peer[2]
            copy = (lambda: remote(part.at[owner], rsbuf.at[k], rs_send, rs_recv, peer).start())
            if ndev > tiles:
                pl.when(owner < tiles)(copy)
            else:
                copy()

        loadings = wide_of(lt)
        noise = jnp.where(iteration == 0, jnp.ones((1, 1), F32), noise_of())
        inverse = inverse_spd(dot_nt(loadings, loadings) + noise * eye)
        at = dot_nn(inverse, loadings)

        if ndev > tiles:
            pl.when(me < tiles)(gather)

            @pl.when(me >= tiles)
            def _():
                wait_all(agbuf, tiles, ag_send, ag_recv).wait_recv()
                wait_all(part, tiles, rs_send, rs_recv).wait_send()
        else:
            gather()

        moment = jnp.concatenate(
            [
                jnp.concatenate([agbuf[i * tile_cols + j] for j in range(tile_cols)], axis=1)
                for i in range(tile_rows)
            ],
            axis=0,
        )
        cross = dot_nn(inverse, moment)
        scaled = (pixels * noise) * inverse + dot_nt(cross, at)
        updated = dot_nn(inverse_spd(scaled), cross)
        crossbuf[...] = cross
        for a in range(naf):
            lt[a] = updated[:, freqs * a : freqs * (a + 1)]
        return carry

    lax.fori_loop(0, ITERS, em_step, 0)
    latg[af] = latent_of(wide_of(lt))

    def lat_copy(k):
        return remote(
            latg.at[af], latg.at[af], lat_send.at[k - 1], lat_recv.at[k - 1],
            (sx, sy, lax.rem(af + k, naf)),
        )

    for k in range(1, naf):
        lat_copy(k).start()
    loadings = wide_of(lt)
    noise = noise_of()
    nv_ref[...] = noise
    lout_ref[...] = lt[af]
    inverse = inverse_spd(dot_nt(loadings, loadings) + noise * eye)
    at_here = dot_nn(inverse, lt[af])
    for k in range(naf):
        if k > 0:
            lat_copy(k).wait_recv()
        g = lax.rem(af - k + naf, naf)
        span = pl.ds(pl.multiple_of(g * gpix, 8), gpix)
        out_ref[span, :] = beamed[span, :] - dot_nn(latg[g].T, at_here)

    for way in range(2):
        @pl.when(y_out[way])
        def _():
            for fb, cg in chunks:
                y_copy(way, fb, cg).wait_send()

        @pl.when(z_out[way])
        def _():
            for fb, cg in chunks:
                z_copy(way, fb, cg).wait_send()
    for k in range(1, naf):
        l_copy(k).wait_send()
        lat_copy(k).wait_send()
        for fb in range(fblocks):
            a_copy(k, fb).wait_send()


def body(sizes, sky_maps, validity, row_taps, column_taps, init_loadings):
    rows, cols, freqs = sky_maps.shape
    comps = init_loadings.shape[1]
    taps = row_taps.shape[1]
    halo = (taps - 1) // 2
    nsx, nsy, naf = sizes
    ndev = nsx * nsy * naf
    tiles = (comps // 8) * (freqs * naf // 128)
    masked = sky_maps * validity.astype(F32)[:, :, None]
    vmem = pl.BlockSpec(memory_space=pltpu.VMEM)
    dma = pltpu.SemaphoreType.DMA
    count = (freqs // 128) * (cols // 8)
    cleaned, loadings, noise = pl.pallas_call(
        functools.partial(kernel, sizes),
        out_shape=(
            jax.ShapeDtypeStruct((rows * cols, freqs), F32),
            jax.ShapeDtypeStruct((comps, freqs), F32),
            jax.ShapeDtypeStruct((1, 1), F32),
        ),
        in_specs=[vmem] * 4,
        out_specs=(vmem, vmem, vmem),
        scratch_shapes=[
            pltpu.VMEM((rows + 2 * halo, cols, freqs), F32),
            pltpu.VMEM((rows, cols + 2 * halo, freqs), F32),
            pltpu.VMEM((taps, 8, freqs), F32),
            pltpu.VMEM((taps, 8, freqs), F32),
            pltpu.VMEM((rows * cols, freqs), F32),
            pltpu.VMEM((naf, rows * cols // naf, freqs), F32),
            pltpu.VMEM((naf, comps, freqs), F32),
            pltpu.VMEM((tiles, 8, 128), F32),
            pltpu.VMEM((ndev, 8, 128), F32),
            pltpu.VMEM((tiles, 8, 128), F32),
            pltpu.VMEM((8, 128), F32),
            pltpu.VMEM((8, 128), F32),
            pltpu.VMEM((ndev, 8, 128), F32),
            pltpu.VMEM((naf, comps, rows * cols // naf), F32),
            pltpu.VMEM((comps, freqs * naf), F32),
            dma((2, count)), dma((2, count)), dma((2, count)), dma((2, count)),
            dma((naf - 1,)), dma((naf - 1,)),
            dma((naf - 1, freqs // 128)), dma((naf - 1, freqs // 128)),
            dma, dma, dma, dma, dma, dma,
            dma((naf - 1,)), dma((naf - 1,)),
        ],
        compiler_params=pltpu.CompilerParams(
            collective_id=0, has_side_effects=True, vmem_limit_bytes=48 * 1024 * 1024
        ),
        name="beam_pca",
    )(masked, row_taps.T, column_taps.T, init_loadings.T)
    return cleaned.reshape(rows, cols, freqs), loadings.T, noise[0, 0]


def solution(mesh):
    sizes = tuple(mesh.shape[axis] for axis in ("sx", "sy", "af"))
    placed = (P("sx", "sy", "af"), P("sx", "sy"), P("af", None), P("af", None), P("af", None))
    return jax.shard_map(
        functools.partial(body, sizes),
        mesh=mesh,
        in_specs=placed,
        out_specs=(P("sx", "sy", "af"), P("af", None), P()),
        check_vma=False,
    )
```
